256 devices in a mesh: dp: 32 (over y, z_lo, core), tensor: 8 (over x, z_hi).
Axes of the slice: x: 4, y: 4, z: 8 (z_hi: 2, z_lo: 4; z = z_hi * 4 + z_lo), core: 2. Of those that a mesh axis runs over, the one named last changes fastest.
Arguments:
- activations: bfloat16 [32768, 8192], P(('dp', 'tensor')), may hold values from -6 to 6
- output_gradient: bfloat16 [32768, 6144], P('dp', 'tensor'), may hold values from -6 to 6
- packed_weight_nibbles: int32 [2048, 6144], P(None, 'tensor'), may hold values from 0 to 65535
- group_scale_table: float32 [64, 6144], P(None, 'tensor'), may hold values from 0.001275776 to 0.005103104
- dense_feature_index: int32 [64], replicated, may hold values from 0 to 8191, as said below
- dense_feature_weight: float32 [64, 6144], P(None, 'tensor'), may hold values from -0.078125 to 0.078125
- adapter_down_weight: bfloat16 [8192, 16], replicated, may hold values from -0.1875 to 0.1875
- adapter_up_weight: bfloat16 [16, 6144], P(None, 'tensor'), may hold values from -0.0390625 to 0.0390625
Outputs:
- layer_input_gradient: bfloat16 [32768, 8192], P(('dp', 'tensor'))
- down_grad: float32 [8192, 16], replicated
- up_weight_gradient: float32 [16, 6144], P(None, 'tensor')
- outlier_grad: float32 [64, 6144], P(None, 'tensor')
The draws below stay inside these ranges and needn't reach their ends.
Inputs may be any that keep to these rules, and one draw needn't show every extreme that they name: `packed_weight_nibbles`: each word holds four codes of 0 to 15 in its four lowest groups of four bits, the lowest group for the first of its four input features; every such bit pattern may occur. `dense_feature_index`: distinct and increasing, one in each aligned block of 128 input features, the first 0 and the last 8191.
All inputs are finite; a program needn't handle non-finite values.
Results may differ from the reference program's by a relative error of at most 0.017.
Values may be sent and summed in bfloat16 or wider, within the bound.
A program may use at most 192 MiB of HBM per device.

```python
import math
import jax
import jax.numpy as jnp
from jax import lax

MODEL_WIDTH = 8192
ADAPTER_RANK = 16
GROUP = 128
K_OUT = 64
TOK_DEV = 128
OUTPUT_FEATURES = 6144
TOKENS = 32768
N_DP = 32
N_TENSOR = 8


def draw_dense_feature_index(key, part):
    key = jax.random.fold_in(key, 11)
    stride = MODEL_WIDTH // K_OUT
    offsets = jax.random.randint(key, (K_OUT,), 0, stride, dtype=jnp.int32)
    offsets = offsets.at[0].set(0).at[K_OUT - 1].set(stride - 1)
    return jnp.arange(K_OUT, dtype=jnp.int32) * stride + offsets


def touch_ends(array, key, least, largest):
    place = [jax.random.randint(jax.random.fold_in(key, axis), (), 0, length) for axis, length in enumerate(array.shape)]
    widest = array.shape.index(max(array.shape))
    neighbour = place[:widest] + [(place[widest] + 1) % array.shape[widest]] + place[widest + 1:]
    return array.at[tuple(place)].set(least).at[tuple(neighbour)].set(largest)


def block_scale(key, extent, split, low, top_value):
    def one(position, blocks):
        steps = jax.random.uniform(jax.random.fold_in(jax.random.fold_in(key, 6), position), (blocks,), jnp.float32, low / len(split), top_value / len(split))
        return jnp.repeat(jnp.exp(steps), extent[position] // blocks).reshape((-1,) + (1,) * (len(extent) - position - 1))

    gain = one(*split[0])
    for cut in split[1:]:
        gain = gain * one(*cut)
    return gain


def scatter_about(rng, shape, width, limit, split=(), kind=jnp.bfloat16):
    factor_of = block_scale(rng, shape, split, -0.22, 0.18) if split else 1.0
    array = jax.random.normal(rng, shape, jnp.float32) * width * factor_of
    return jnp.minimum(jnp.maximum(array, -limit), limit).astype(kind)


def setup_inputs(seed: int = 0) -> dict:
    splits = jax.random.split(jax.random.key(seed), 9)
    return {
        "activations": scatter_about(splits[0], (TOKENS, MODEL_WIDTH), 1.0, 6.0, ((0, 256),)),
        "output_gradient": scatter_about(splits[1], (TOKENS, OUTPUT_FEATURES), 1.0, 6.0, ((0, 32), (1, 8))),
        "packed_weight_nibbles": touch_ends(jax.random.randint(splits[2], (MODEL_WIDTH // 4, OUTPUT_FEATURES), 0, 65536), jax.random.fold_in(splits[2], 1), 0, 65535).astype(jnp.int32),
        "group_scale_table": jnp.clip(jnp.exp(math.log(0.005103104) - 1.3862944 * jax.random.uniform(splits[3], (MODEL_WIDTH // GROUP, OUTPUT_FEATURES), jnp.float32) ** block_scale(splits[3], (MODEL_WIDTH // GROUP, OUTPUT_FEATURES), ((1, 8),), -0.2, 0.2)), 0.001275776, 0.005103104),
        "dense_feature_index": draw_dense_feature_index(jax.random.fold_in(splits[8], 71), 0),
        "dense_feature_weight": scatter_about(splits[5], (K_OUT, OUTPUT_FEATURES), OUTPUT_FEATURES ** -0.5, 0.078125, ((1, 8),), jnp.float32),
        "adapter_down_weight": scatter_about(splits[6], (MODEL_WIDTH, ADAPTER_RANK), (ADAPTER_RANK * 64) ** -0.5, 0.1875),
        "adapter_up_weight": scatter_about(splits[7], (ADAPTER_RANK, OUTPUT_FEATURES), (4 * OUTPUT_FEATURES) ** -0.5, 0.0390625, ((1, 8),)),
    }


ADAPTER_SCALE = 2.0

def unpack(packed_weight_nibbles, group_scale_table):
    packed_rows = packed_weight_nibbles.shape[0]
    columns = packed_weight_nibbles.shape[1]
    total_rows = packed_rows * 4
    blocks = packed_weight_nibbles.reshape(total_rows // GROUP, GROUP // 4, columns)
    shifts = 4 * jnp.arange(4, dtype=jnp.int32)

    def one_group(pair):
        packed, scale_row = pair
        nibbles = jnp.bitwise_and(jnp.right_shift(packed[:, None, :], shifts[None, :, None]), 15)
        values = (nibbles.astype(jnp.float32) - 8.0) * scale_row[None, None, :]
        return values.reshape(GROUP, columns).astype(jnp.bfloat16)
    return lax.map(one_group, (blocks, group_scale_table)).reshape(total_rows, columns)

def reference(activations, output_gradient, packed_weight_nibbles, group_scale_table, dense_feature_index, dense_feature_weight, adapter_down_weight, adapter_up_weight):
    group_rows = TOK_DEV * N_TENSOR
    shard_cols = OUTPUT_FEATURES // N_TENSOR
    grad_norm = float(TOKENS) ** (-0.5)
    weight = unpack(packed_weight_nibbles, group_scale_table)
    rank_gradient = (ADAPTER_SCALE * jnp.dot(output_gradient, adapter_up_weight.T, preferred_element_type=jnp.float32)).astype(jnp.bfloat16)

    def group_grad(pair):
        gradient_rows, rank_row_values = pair
        reduced_sum = jnp.zeros((group_rows, MODEL_WIDTH), jnp.float32)
        for shard in range(N_TENSOR):
            grad_cols = gradient_rows[:, shard * shard_cols:(shard + 1) * shard_cols]
            partial_value = jnp.dot(grad_cols, weight[:, shard * shard_cols:(shard + 1) * shard_cols].T, preferred_element_type=jnp.float32)
            outlier_term = jnp.dot(grad_cols.astype(jnp.float32), dense_feature_weight[:, shard * shard_cols:(shard + 1) * shard_cols].T, precision=lax.Precision.HIGHEST)
            partial_value = partial_value.at[:, dense_feature_index].add(outlier_term)
            rounded = lax.optimization_barrier(partial_value.astype(jnp.bfloat16))
            reduced_sum = reduced_sum + rounded.astype(jnp.float32)
        reduced_sum = reduced_sum + jnp.dot(rank_row_values, adapter_down_weight.T, preferred_element_type=jnp.float32)
        return reduced_sum.astype(jnp.bfloat16)
    layer_input_gradient = lax.map(group_grad, (output_gradient.reshape(N_DP, group_rows, OUTPUT_FEATURES), rank_gradient.reshape(N_DP, group_rows, ADAPTER_RANK))).reshape(TOKENS, MODEL_WIDTH)
    hidden_state = jnp.dot(activations, adapter_down_weight, preferred_element_type=jnp.float32).astype(jnp.bfloat16)
    up_weight_gradient = ADAPTER_SCALE * grad_norm * jnp.dot(hidden_state.T, output_gradient, preferred_element_type=jnp.float32)
    outlier_grad = grad_norm * jnp.dot(activations[:, dense_feature_index].T, output_gradient, preferred_element_type=jnp.float32)
    down_grad = grad_norm * jnp.dot(activations.T, rank_gradient, preferred_element_type=jnp.float32)
    return (layer_input_gradient, down_grad, up_weight_gradient, outlier_grad)
```

```python
import functools

import jax
import jax.numpy as jnp
from jax import lax
from jax.experimental import pallas as pl
from jax.experimental.pallas import tpu as pltpu
from jax.sharding import PartitionSpec as P

MESH = pl.DeviceIdType.MESH
F32 = jnp.float32
BF16 = jnp.bfloat16

WIDTH = 8192
FEATS = 768
RANK = 16
KOUT = 64
TOK = 128
GROUP = 128
DC = 512
NC = WIDTH // DC
GPC = DC // GROUP
PR = DC // 4
HROWS = 96
NORM = 32768.0**-0.5


def mm(a, b, ca, cb):
    return lax.dot_general(a, b, (((ca,), (cb,)), ((), ())), preferred_element_type=F32)


def iota(shape, dim):
    return lax.broadcasted_iota(jnp.int32, shape, dim)


def eye(n):
    return (iota((n, n), 0) == iota((n, n), 1)).astype(BF16)


def unshuffle():
    q, d = iota((GROUP, GROUP), 0), iota((GROUP, GROUP), 1)
    return (d == 4 * (q & 31) + (q >> 5)).astype(BF16)


def kernel(
    act_h, g_h, pk_h, scale, idx, dfw, a_h, up,
    out_h, out_d, out_u, out_o,
    act, g, pk, a_v, at, w, rank, rank_in, r_v, hid, dsum, dbuf, dall, usum, ubuf, uall,
    s1, r1, s2, r2, sz, rz, own, outv,
    l_sem, pk_sem, o_sem, s1s, s1r, s2s, s2r, zs, zr, rks, rkr, hs, hr, ds, dr, us, ur,
):
    dp = lax.axis_index("dp")
    t = lax.axis_index("tensor")
    core = lax.rem(dp, 2)
    y = dp // 8
    zl = lax.rem(dp // 2, 4)
    x = t // 2
    zh = lax.rem(t, 2)
    z = zh * 4 + zl

    def at_t(d):
        return (dp, lax.rem(t + d, 8))

    def at_x(d):
        return (dp, lax.rem(x + d + 4, 4) * 2 + zh)

    def at_y(d):
        return ((lax.rem(y + d, 4) * 4 + zl) * 2 + core, t)

    def at_z(d):
        zz = lax.rem(z + d, 8)
        return ((y * 4 + lax.rem(zz, 4)) * 2 + core, x * 2 + zz // 4)

    def at_zl(d):
        return ((y * 4 + lax.rem(zl + d, 4)) * 2 + core, t)

    sibling = (dp + 1 - 2 * core, t)

    def rc(src, dst, ssem, rsem, dev):
        return pltpu.make_async_remote_copy(
            src_ref=src, dst_ref=dst, send_sem=ssem, recv_sem=rsem,
            device_id=dev, device_id_type=MESH,
        )

    bar = pltpu.get_barrier_semaphore()
    peers = [at_t(d) for d in range(1, 8)]
    peers += [at_y(d) for d in range(1, 4)]
    peers += [at_z(d) for d in (1, 2, 3, 5, 6, 7)]
    peers += [sibling]
    for dev in peers:
        pl.semaphore_signal(bar, inc=1, device_id=dev, device_id_type=MESH)

    cp_g = pltpu.make_async_copy(g_h, g, l_sem.at[0])
    cp_act = pltpu.make_async_copy(act_h, act, l_sem.at[1])
    cp_a = pltpu.make_async_copy(a_h, a_v, l_sem.at[2])

    def cp_pk(j):
        return pltpu.make_async_copy(
            pk_h.at[pl.ds(j * PR, PR)], pk.at[j], pk_sem.at[j]
        )

    cp_g.start()
    for j in range(2):
        cp_pk(j).start()
    cp_act.start()
    cp_a.start()
    for j in range(2, NC):
        cp_pk(j).start()
    cp_g.wait()

    def unpack(j):
        cp_pk(j).wait()
        slot = lax.rem(j, 3)
        for q in range(GPC):
            k = j * GPC + q
            words = pk[j, pl.ds(q * 32, 32), :]
            srow = scale[pl.ds(k, 1), :]
            drow = dfw[pl.ds(k, 1), :]
            place = idx[pl.ds(k, 1), :] - k * GROUP
            place = (place & 3) * 32 + (place >> 2)
            for n in range(4):
                code = lax.shift_right_logical(words, 4 * n) & 15
                val = (code.astype(F32) - 8.0) * srow
                hit = iota((32, FEATS), 0) + n * 32 == place
                val = val + jnp.where(hit, drow, 0.0)
                w[slot, pl.ds(q * GROUP + n * 32, 32), :] = val.astype(BF16)

    def part(j, xx):
        rows = g[pl.ds(pl.multiple_of(xx * 256, 256), 256), :]
        return mm(rows, w[lax.rem(j, 3)], 1, 1)

    def c1(j, i):
        return rc(s1.at[j, i], r1.at[j, i], s1s.at[j, i], s1r.at[j, i], at_x(1 - 2 * i))

    def c2(j, i):
        return rc(s2.at[j, i], r2.at[j, i], s2s.at[j, i], s2r.at[j, i], at_x(1 - 2 * i))

    def cz(j):
        return rc(sz.at[j], rz.at[j], zs.at[j], zr.at[j], at_z(4))

    def stage1(j):
        p = part(j, lax.rem(x + 2, 4)).astype(BF16)
        s1[j, 0] = p[:TOK]
        s1[j, 1] = p[TOK:]

    def stage2(j):
        for i in range(2):
            p = part(j, lax.rem(x + 5 - 2 * i, 4))
            c1(j, i).wait_recv()
            got = r1[j, i].astype(F32)
            lo, hi = p[:TOK], p[TOK:]
            if i == 0:
                lo = lo + got
            else:
                hi = hi + got
            s2[j, i, pl.ds(0, TOK), :] = lo.astype(BF16)
            s2[j, i, pl.ds(TOK, TOK), :] = hi.astype(BF16)
            c2(j, i).start()

    def stage3(j):
        p = part(j, x)
        c2(j, 0).wait_recv()
        c2(j, 1).wait_recv()
        p = p + r2[j, 0].astype(F32) + r2[j, 1].astype(F32)
        first = zh == 0
        own[j] = jnp.where(first, p[:TOK], p[TOK:])
        sz[j] = jnp.where(first, p[TOK:], p[:TOK]).astype(BF16)
        cz(j).start()

    def out_copy(j):
        cols = pl.ds(pl.multiple_of(j * DC, DC), DC)
        return pltpu.make_async_copy(outv.at[j], out_h.at[:, cols], o_sem.at[j])

    def stage4(j):
        shuf = unshuffle()
        cols = at[:, pl.ds(pl.multiple_of(j * DC, DC), DC)]
        cz(j).wait_recv()
        for q in range(GPC):
            lanes = slice(q * GROUP, (q + 1) * GROUP)
            a_q = mm(cols[:, lanes], shuf, 1, 1).astype(BF16)
            total = own[j, :, lanes] + rz[j, :, lanes].astype(F32)
            total = total + mm(r_v[...], a_q, 1, 0)
            outv[j, :, lanes] = mm(total.astype(BF16), shuf, 1, 0).astype(BF16)
        out_copy(j).start()

    def c_rank(d):
        return rc(rank.at[lax.rem(t + d, 8)], rank_in.at[t], rks.at[d], rkr.at[d], at_t(d))

    def c_hid(d):
        return rc(hid.at[t], hid.at[t], hs.at[d], hr.at[d], at_t(d))

    def cd_core():
        return rc(dsum.at[1 - core], dbuf.at[pl.ds(0, 16)], ds.at[0], dr.at[0], sibling)

    def cu_core():
        return rc(usum.at[1 - core], ubuf.at[pl.ds(0, 4)], us.at[0], ur.at[0], sibling)

    def cd_x(d):
        to = lax.rem(x + d, 4)
        src = dsum.at[core, pl.ds(to * 4, 4)]
        return rc(src, dbuf.at[pl.ds(16 + 4 * (d - 1), 4)], ds.at[d], dr.at[d], at_x(d))

    def cd_y(d):
        src = dsum.at[core, x * 4 + lax.rem(y + d, 4)]
        return rc(src, dbuf.at[28 + d - 1], ds.at[3 + d], dr.at[3 + d], at_y(d))

    def cd_z(d):
        return rc(dbuf.at[31 + z], dbuf.at[31 + z], ds.at[6 + d], dr.at[6 + d], at_z(d))

    def cu_y(d):
        src = usum.at[core, lax.rem(y + d, 4)]
        return rc(src, ubuf.at[4 + d - 1], us.at[d], ur.at[d], at_y(d))

    def cu_z(d):
        return rc(ubuf.at[7 + zl], ubuf.at[7 + zl], us.at[3 + d], ur.at[3 + d], at_zl(d))

    def cd_gy(d):
        ref = dall.at[core, x * 4 + y]
        return rc(ref, ref, ds.at[13 + d], dr.at[13 + d], at_y(d))

    def cd_gx(d):
        ref = dall.at[core, pl.ds(x * 4, 4)]
        return rc(ref, ref, ds.at[16 + d], dr.at[16 + d], at_x(d))

    def cd_gc():
        ref = dall.at[core]
        return rc(ref, ref, ds.at[20], dr.at[20], sibling)

    def cu_gy(d):
        ref = uall.at[core, y]
        return rc(ref, ref, us.at[6 + d], ur.at[6 + d], at_y(d))

    def cu_gc():
        ref = uall.at[core]
        return rc(ref, ref, us.at[10], ur.at[10], sibling)

    r13, r17 = range(1, 4), range(1, 8)

    def small0():
        part_r = mm(up[...], g[...], 1, 1)
        for k in range(8):
            rank[k] = part_r[:, k * TOK:(k + 1) * TOK]
        rank_in[t] = rank[t]
        for d in r17:
            c_rank(d).start()
        cp_act.wait()
        cp_a.wait()
        e16 = eye(RANK)
        total = jnp.zeros((HROWS, TOK), F32)
        step = 1024
        for c in range(WIDTH // step):
            cols = slice(c * step, (c + 1) * step)
            a_c = mm(e16, a_v[cols, :], 1, 1).astype(BF16)
            at[:, cols] = a_c
            hot = (iota((KOUT, step), 1) + c * step == idx[...]).astype(F32).astype(BF16)
            zero = jnp.zeros((HROWS - RANK - KOUT, step), BF16)
            basis = jnp.concatenate([a_c, hot, zero], axis=0)
            total = total + mm(basis, act[:, cols], 1, 1)
        hid[t] = total.astype(BF16)
        for d in r17:
            c_hid(d).start()

    def small1():
        for d in r17:
            c_rank(d).wait_recv()
        total = rank_in[0]
        for k in range(1, 8):
            total = total + rank_in[k]
        r_t = (2.0 * total).astype(BF16)
        r_v[...] = mm(eye(TOK), r_t, 1, 1).astype(BF16)
        for k in range(32):
            cols = slice(k * 256, (k + 1) * 256)
            dsum[k // 16, k % 16] = mm(r_t, act[:, cols], 1, 0)
        cd_core().start()

    def small2():
        for d in r17:
            c_hid(d).wait_recv()
        total = jnp.zeros((HROWS, FEATS), F32)
        for k in range(8):
            total = total + mm(hid[k], g[k * TOK:(k + 1) * TOK, :], 1, 0)
        for c in range(2):
            for k in range(4):
                usum[c, k] = total[k * 24:(k + 1) * 24, c * 384:(c + 1) * 384]
        cu_core().start()

    def small3():
        cd_core().wait_recv()
        for k in range(16):
            dsum[core, k] = dsum[core, k] + dbuf[k]
        for d in r13:
            cd_x(d).start()
        cu_core().wait_recv()
        for k in range(4):
            usum[core, k] = usum[core, k] + ubuf[k]
        for d in r13:
            cu_y(d).start()

    def small4():
        for d in r13:
            cd_x(d).wait_recv()
        for k in range(4):
            mine = dsum[core, x * 4 + k]
            for d in r13:
                mine = mine + dbuf[16 + 4 * (d - 1) + k]
            dsum[core, x * 4 + k] = mine
        for d in r13:
            cd_y(d).start()
        for d in r13:
            cu_y(d).wait_recv()
        mine = usum[core, y]
        for d in r13:
            mine = mine + ubuf[4 + d - 1]
        ubuf[7 + zl] = mine
        for d in r13:
            cu_z(d).start()

    def small5():
        for d in r13:
            cd_y(d).wait_recv()
        mine = dsum[core, x * 4 + y]
        for d in r13:
            mine = mine + dbuf[28 + d - 1]
        dbuf[31 + z] = mine
        for d in r17:
            cd_z(d).start()
        for d in r13:
            cu_z(d).wait_recv()
        total = ubuf[7]
        for k in r13:
            total = total + ubuf[7 + k]
        uall[core, y] = total
        for d in r13:
            cu_gy(d).start()

    def small6():
        for d in r17:
            cd_z(d).wait_recv()
        total = dbuf[31]
        for k in range(1, 8):
            total = total + dbuf[31 + k]
        dall[core, x * 4 + y] = total * NORM
        for d in r13:
            cd_gy(d).start()
        for d in r13:
            cu_gy(d).wait_recv()
        cu_gc().start()

    def small7():
        for d in r13:
            cd_gy(d).wait_recv()
        for d in r13:
            cd_gx(d).start()
        cu_gc().wait_recv()
        for c in range(2):
            lanes = slice(c * 384, (c + 1) * 384)
            u0 = uall[c, 0]
            out_u[:, lanes] = u0[:16] * (2.0 * NORM)
            out_o[0:8, lanes] = u0[16:] * NORM
            out_o[8:32, lanes] = uall[c, 1] * NORM
            out_o[32:56, lanes] = uall[c, 2] * NORM
            out_o[56:64, lanes] = uall[c, 3, :8] * NORM

    def small8():
        for d in r13:
            cd_gx(d).wait_recv()
        cd_gc().start()

    def small9():
        cd_gc().wait_recv()
        for c in range(2):
            for k in range(16):
                out_d[c * 16 + k] = dall[c, k]

    unpack(0)
    stage1(0)
    pl.semaphore_wait(bar, len(peers))
    for i in range(2):
        c1(0, i).start()
    small0()

    small = {2: small1, 3: small2, 4: small3, 5: small4, 6: small5, 7: small6,
             8: small7, 9: small8, 10: small9}

    def step(j, carry):
        @pl.when(j < NC)
        def _():
            unpack(j)
            stage1(j)
            for i in range(2):
                c1(j, i).start()

        @pl.when(j <= NC)
        def _():
            stage2(j - 1)

        @pl.when((j >= 2) & (j <= NC + 1))
        def _():
            stage3(j - 2)

        @pl.when(j >= 4)
        def _():
            stage4(j - 4)

        for at_step, piece in small.items():
            pl.when(j == at_step)(piece)
        return carry

    lax.fori_loop(1, NC + 4, step, 0)

    def drain(j, carry):
        for i in range(2):
            c1(j, i).wait_send()
            c2(j, i).wait_send()
        cz(j).wait_send()
        out_copy(j).wait()
        return carry

    lax.fori_loop(0, NC, drain, 0)
    for d in r17:
        c_rank(d).wait_send()
        c_hid(d).wait_send()
        cd_z(d).wait_send()
    for d in r13:
        cd_x(d).wait_send()
        cd_y(d).wait_send()
        cu_y(d).wait_send()
        cu_z(d).wait_send()
        cd_gy(d).wait_send()
        cd_gx(d).wait_send()
        cu_gy(d).wait_send()
    cd_core().wait_send()
    cu_core().wait_send()
    cd_gc().wait_send()
    cu_gc().wait_send()


def body(act, g, pk, scale, idx, dfw, a, up):
    hbm = pl.BlockSpec(memory_space=pl.ANY)
    vmem = pl.BlockSpec(memory_space=pltpu.VMEM)
    dma = pltpu.SemaphoreType.DMA
    out, d, u, o = pl.pallas_call(
        kernel,
        out_shape=(
            jax.ShapeDtypeStruct((TOK, WIDTH), BF16),
            jax.ShapeDtypeStruct((32, RANK, 256), F32),
            jax.ShapeDtypeStruct((RANK, FEATS), F32),
            jax.ShapeDtypeStruct((KOUT, FEATS), F32),
        ),
        in_specs=[hbm, hbm, hbm, vmem, vmem, vmem, hbm, vmem],
        out_specs=(hbm, vmem, vmem, vmem),
        scratch_shapes=[
            pltpu.VMEM((TOK, WIDTH), BF16),
            pltpu.VMEM((8 * TOK, FEATS), BF16),
            pltpu.VMEM((NC, PR, FEATS), jnp.int32),
            pltpu.VMEM((WIDTH, RANK), BF16),
            pltpu.VMEM((RANK, WIDTH), BF16),
            pltpu.VMEM((3, DC, FEATS), BF16),
            pltpu.VMEM((8, RANK, TOK), F32),
            pltpu.VMEM((8, RANK, TOK), F32),
            pltpu.VMEM((TOK, RANK), BF16),
            pltpu.VMEM((8, HROWS, TOK), BF16),
            pltpu.VMEM((2, 16, RANK, 256), F32),
            pltpu.VMEM((39, RANK, 256), F32),
            pltpu.VMEM((2, 16, RANK, 256), F32),
            pltpu.VMEM((2, 4, 24, 384), F32),
            pltpu.VMEM((11, 24, 384), F32),
            pltpu.VMEM((2, 4, 24, 384), F32),
            pltpu.VMEM((NC, 2, TOK, DC), BF16),
            pltpu.VMEM((NC, 2, TOK, DC), BF16),
            pltpu.VMEM((NC, 2, 2 * TOK, DC), BF16),
            pltpu.VMEM((NC, 2, 2 * TOK, DC), BF16),
            pltpu.VMEM((NC, TOK, DC), BF16),
            pltpu.VMEM((NC, TOK, DC), BF16),
            pltpu.VMEM((NC, TOK, DC), F32),
            pltpu.VMEM((NC, TOK, DC), BF16),
            dma((3,)), dma((NC,)), dma((NC,)),
            dma((NC, 2)), dma((NC, 2)), dma((NC, 2)), dma((NC, 2)),
            dma((NC,)), dma((NC,)),
            dma((8,)), dma((8,)), dma((8,)), dma((8,)),
            dma((21,)), dma((21,)), dma((11,)), dma((11,)),
        ],
        compiler_params=pltpu.CompilerParams(
            collective_id=0, has_side_effects=True, vmem_limit_bytes=60 << 20
        ),
        name="projection_backward",
    )(act, g, pk, scale, idx.reshape(KOUT, 1), dfw, a, up)
    return out, d.transpose(0, 2, 1).reshape(WIDTH, RANK), u, o


def solution(mesh):
    tensor = P(None, "tensor")
    tokens = P(("dp", "tensor"), None)
    return jax.shard_map(
        body,
        mesh=mesh,
        in_specs=(tokens, P("dp", "tensor"), tensor, tensor, P(), tensor, P(), tensor),
        out_specs=(tokens, P(), tensor, tensor),
        check_vma=False,
    )
```

```python
import functools

import jax
import jax.numpy as jnp
from jax import lax
from jax.experimental import pallas as pl
from jax.experimental.pallas import tpu as pltpu
from jax.sharding import PartitionSpec as P

MESH = pl.DeviceIdType.MESH
F32 = jnp.float32
BF16 = jnp.bfloat16

WIDTH = 8192
FEATS = 768
RANK = 16
KOUT = 64
TOK = 128
GROUP = 128
DC = 512
NC = WIDTH // DC
GPC = DC // GROUP
PR = DC // 4
NA = 7
NB = NC - NA
S2 = 2
S3 = 4
CUTS = (0, 2, 5, 9)
PK = 6
HROWS = 96
NORM = 32768.0**-0.5


def mm(a, b, ca, cb):
    return lax.dot_general(a, b, (((ca,), (cb,)), ((), ())), preferred_element_type=F32)


def iota(shape, dim):
    return lax.broadcasted_iota(jnp.int32, shape, dim)


def eye(n):
    return (iota((n, n), 0) == iota((n, n), 1)).astype(BF16)


def unshuffle():
    q, d = iota((GROUP, GROUP), 0), iota((GROUP, GROUP), 1)
    return (d == 4 * (q & 31) + (q >> 5)).astype(BF16)


def kernel(
    act_h, g_h, pk_h, scale, idx_row, dfw, at, up,
    out_h, out_d, out_u, out_o,
    act, g, gb, gp, pka, pkb, idx, atp, w, wp, rank, rank_in, r_v, hid, dsum, dbuf, dall, usum, ubuf, uall,
    s1, r1, s2, r2, sz, rz, own, t1, q1, t2, q2, near, home, outv,
    l_sem, pka_sem, pkb_sem, o_sem, s1s, s1r, s2s, s2r, zs, zr, t1s, t1r, t2s, t2r, gs, gr,
    wzs, wzr, wfs, wys, wyr, wcs, wcr, rks, rkr, hs, hr, ds, dr, us, ur,
):
    dp = lax.axis_index("dp")
    t = lax.axis_index("tensor")
    core = lax.rem(dp, 2)
    y = dp // 8
    zl = lax.rem(dp // 2, 4)
    x = t // 2
    zh = lax.rem(t, 2)
    z = zh * 4 + zl

    def at_t(d):
        return (dp, lax.rem(t + d, 8))

    def at_x(d):
        return (dp, lax.rem(x + d + 4, 4) * 2 + zh)

    def at_y(d):
        return ((lax.rem(y + d, 4) * 4 + zl) * 2 + core, t)

    def at_z(d):
        zz = lax.rem(z + d, 8)
        return ((y * 4 + lax.rem(zz, 4)) * 2 + core, x * 2 + zz // 4)

    def at_zl(d):
        return ((y * 4 + lax.rem(zl + d, 4)) * 2 + core, t)

    sibling = (dp + 1 - 2 * core, t)

    def rc(src, dst, ssem, rsem, dev):
        return pltpu.make_async_remote_copy(
            src_ref=src, dst_ref=dst, send_sem=ssem, recv_sem=rsem,
            device_id=dev, device_id_type=MESH,
        )

    bar = pltpu.get_barrier_semaphore()
    peers = [at_t(d) for d in range(1, 8)]
    peers += [at_y(d) for d in range(1, 4)]
    peers += [at_z(d) for d in (1, 2, 3, 5, 6, 7)]
    peers += [sibling]
    for dev in peers:
        pl.semaphore_signal(bar, inc=1, device_id=dev, device_id_type=MESH)

    cp_g = pltpu.make_async_copy(g_h, g, l_sem.at[0])
    cp_act = pltpu.make_async_copy(act_h, act, l_sem.at[1])

    def cp_a(j):
        return pltpu.make_async_copy(pk_h.at[pl.ds(j * PR, PR)], pka.at[j], pka_sem.at[j])

    def cp_b(b):
        slot = lax.rem(b, PK)
        src = pk_h.at[pl.ds((NA + b) * PR, PR)]
        return pltpu.make_async_copy(src, pkb.at[slot], pkb_sem.at[slot])

    cp_g.start()
    cp_a(0).start()
    cp_b(0).start()
    for j in range(1, NA):
        cp_a(j).start()
    cp_act.start()
    for b in range(1, PK):
        cp_b(b).start()
    row = idx_row[...].astype(F32)
    idx[...] = jnp.sum(
        jnp.where(iota((KOUT, KOUT), 0) == iota((KOUT, KOUT), 1), row, 0.0),
        axis=1, keepdims=True,
    ).astype(jnp.int32)

    def unpack(j, packed):
        for q in range(GPC):
            k = j * GPC + q
            words = packed[pl.ds(q * 32, 32), :]
            srow = scale[pl.ds(k, 1), :]
            drow = dfw[pl.ds(k, 1), :]
            place = idx[pl.ds(k, 1), :] - k * GROUP
            place = (place & 3) * 32 + (place >> 2)
            for n in range(4):
                code = lax.shift_right_logical(words, 4 * n) & 15
                val = (code.astype(F32) - 8.0) * srow
                hit = iota((32, FEATS), 0) + n * 32 == place
                val = val + jnp.where(hit, drow, 0.0)
                w[j, pl.ds(q * GROUP + n * 32, 32), :] = val.astype(BF16)

    def unpack_a(j):
        cp_a(j).wait()
        unpack(j, pka.at[j])

    def unpack_b(b):
        cp_b(b).wait()
        unpack(NA + b, pkb.at[lax.rem(b, PK)])

        @pl.when(b + PK < NB)
        def _():
            cp_b(b + PK).start()

    def part(j, xx):
        rows = g[pl.ds(pl.multiple_of(xx * 256, 256), 256), :]
        return mm(rows, w[j], 1, 1)

    def c1(j, i):
        return rc(s1.at[j, i], r1.at[j, i], s1s.at[j, i], s1r.at[j, i], at_x(1 - 2 * i))

    def c2(j, i):
        return rc(s2.at[j, i], r2.at[j, i], s2s.at[j, i], s2r.at[j, i], at_x(1 - 2 * i))

    def cz(j):
        return rc(sz.at[j], rz.at[j], zs.at[j], zr.at[j], at_z(4))

    def stage1(j):
        p = part(j, lax.rem(x + 2, 4)).astype(BF16)
        s1[j, 0] = p[:TOK]
        s1[j, 1] = p[TOK:]

    def stage2(j):
        for i in range(2):
            p = part(j, lax.rem(x + 5 - 2 * i, 4))
            c1(j, i).wait_recv()
            got = r1[j, i].astype(F32)
            lo, hi = p[:TOK], p[TOK:]
            if i == 0:
                lo = lo + got
            else:
                hi = hi + got
            s2[j, i, pl.ds(0, TOK), :] = lo.astype(BF16)
            s2[j, i, pl.ds(TOK, TOK), :] = hi.astype(BF16)
            c2(j, i).start()

    def stage3(j):
        p = part(j, x)
        c2(j, 0).wait_recv()
        c2(j, 1).wait_recv()
        p = p + r2[j, 0].astype(F32) + r2[j, 1].astype(F32)
        first = zh == 0
        own[j] = jnp.where(first, p[:TOK], p[TOK:])
        sz[j] = jnp.where(first, p[TOK:], p[:TOK]).astype(BF16)

    def out_copy(j):
        cols = pl.ds(pl.multiple_of(j * DC, DC), DC)
        return pltpu.make_async_copy(outv.at[j], out_h.at[:, cols], o_sem.at[j])

    def finish(j, total):
        shuf = unshuffle()
        cols = atp[:, pl.ds(pl.multiple_of(j * DC, DC), DC)]
        full = (total + mm(r_v[...], cols, 1, 0)).astype(BF16)
        for q in range(GPC):
            lanes = slice(q * GROUP, (q + 1) * GROUP)
            outv[j, :, lanes] = mm(full[:, lanes], shuf, 1, 0).astype(BF16)
        out_copy(j).start()

    def stage4(j):
        cz(j).wait_recv()
        finish(j, own[j] + rz[j].astype(F32))

    order = (2, 1, 3, 0)

    def block(d, half):
        return pl.ds(pl.multiple_of((lax.rem(x + d, 4) * 2 + half) * TOK, TOK), TOK)

    def c_g(k):
        dst = gp.at[pl.ds(k * TOK, TOK)]
        return rc(g.at[block(order[k], 1 - zh)], dst, gs.at[k], gr.at[k], at_z(4))

    def piece(b, k):
        return wp.at[b, pl.ds(pl.multiple_of(core * 256 + k * 64, 64), 64)]

    outer = (zl == 0) | (zl == 3)

    def c_wz(b):
        src = w.at[NA + b, pl.ds(pl.multiple_of(core * 256 + y * 64, 64), 64)]
        return rc(src, piece(b, y), wzs.at[b], wzr.at[b], at_z(7 - 2 * zl))

    def c_wf(b):
        return rc(piece(b, y), piece(b, y), wfs.at[b], wzr.at[b], at_z(1 + 2 * zl))

    def c_wy(b, d):
        return rc(piece(b, y), piece(b, y), wys.at[b, d - 1], wyr.at[b, d - 1], at_y(d))

    def c_wc(b):
        ref = wp.at[b, pl.ds(pl.multiple_of(core * 256, 256), 256)]
        return rc(ref, ref, wcs.at[b], wcr.at[b], sibling)

    def spread(b):
        c_wz(b).wait_recv()
        for d in (1, 3, 2):
            c_wy(b, d).start()

    def weight_send(b):
        pl.when(outer)(lambda: c_wz(b).start())

    def weight_on(b):
        @pl.when(outer)
        def _():
            c_wz(b).wait_recv()
            c_wf(b).start()
            for d in (1, 3, 2):
                c_wy(b, d).start()

    def weight_in(b):
        pl.when(jnp.logical_not(outer))(lambda: spread(b))

    def weight_pair(b):
        for d in (1, 3, 2):
            c_wy(b, d).wait_recv()
        c_wc(b).start()

    def d1(b, i):
        return rc(t1.at[b, i], q1.at[b, i], t1s.at[b, i], t1r.at[b, i], at_x(1 - 2 * i))

    def d2(b, i):
        return rc(t2.at[b, i], q2.at[b, i], t2s.at[b, i], t2r.at[b, i], at_x(1 - 2 * i))

    def both1(b):
        c_wc(b).wait_recv()
        p = mm(gb[...], w[NA + b], 1, 1) + mm(gp[...], wp[b], 1, 1)
        far = p[:TOK].astype(BF16)
        t1[b, 0] = far[:64]
        t1[b, 1] = far[64:]
        near[lax.rem(b, S2 + 1)] = p[TOK:3 * TOK]
        home[lax.rem(b, S3 + 1)] = p[3 * TOK:]
        for i in range(2):
            d1(b, i).start()

    def both2(b):
        p = near[lax.rem(b, S2 + 1)]
        d1(b, 0).wait_recv()
        t2[b, 0, pl.ds(0, 64), :] = (p[:64] + q1[b, 0].astype(F32)).astype(BF16)
        t2[b, 0, pl.ds(64, 64), :] = p[64:128].astype(BF16)
        d2(b, 0).start()
        d1(b, 1).wait_recv()
        t2[b, 1, pl.ds(0, 64), :] = p[128:192].astype(BF16)
        t2[b, 1, pl.ds(64, 64), :] = (p[192:] + q1[b, 1].astype(F32)).astype(BF16)
        d2(b, 1).start()

    def both3(b):
        p = home[lax.rem(b, S3 + 1)]
        d2(b, 0).wait_recv()
        d2(b, 1).wait_recv()
        finish(NA + b, p + q2[b, 0].astype(F32) + q2[b, 1].astype(F32))

    def c_rank(d):
        return rc(rank.at[lax.rem(t + d, 8)], rank_in.at[t], rks.at[d], rkr.at[d], at_t(d))

    def c_hid(d):
        return rc(hid.at[t], hid.at[t], hs.at[d], hr.at[d], at_t(d))

    def cd_core():
        return rc(dsum.at[1 - core], dbuf.at[pl.ds(0, 16)], ds.at[0], dr.at[0], sibling)

    def cu_core():
        return rc(usum.at[1 - core], ubuf.at[pl.ds(0, 4)], us.at[0], ur.at[0], sibling)

    def cd_x(d):
        to = lax.rem(x + d, 4)
        src = dsum.at[core, pl.ds(to * 4, 4)]
        return rc(src, dbuf.at[pl.ds(16 + 4 * (d - 1), 4)], ds.at[d], dr.at[d], at_x(d))

    def cd_y(d):
        src = dsum.at[core, x * 4 + lax.rem(y + d, 4)]
        return rc(src, dbuf.at[28 + d - 1], ds.at[3 + d], dr.at[3 + d], at_y(d))

    def cd_z(d):
        return rc(dbuf.at[31 + z], dbuf.at[31 + z], ds.at[6 + d], dr.at[6 + d], at_z(d))

    def cu_y(d):
        src = usum.at[core, lax.rem(y + d, 4)]
        return rc(src, ubuf.at[4 + d - 1], us.at[d], ur.at[d], at_y(d))

    def cu_z(d):
        return rc(ubuf.at[7 + zl], ubuf.at[7 + zl], us.at[3 + d], ur.at[3 + d], at_zl(d))

    def cd_gy(d):
        ref = dall.at[core, x * 4 + y]
        return rc(ref, ref, ds.at[13 + d], dr.at[13 + d], at_y(d))

    def cd_gx(d):
        ref = dall.at[core, pl.ds(x * 4, 4)]
        return rc(ref, ref, ds.at[16 + d], dr.at[16 + d], at_x(d))

    def cd_gc():
        ref = dall.at[core]
        return rc(ref, ref, ds.at[20], dr.at[20], sibling)

    def cu_gy(d):
        ref = uall.at[core, y]
        return rc(ref, ref, us.at[6 + d], ur.at[6 + d], at_y(d))

    def cu_gc():
        ref = uall.at[core]
        return rc(ref, ref, us.at[10], ur.at[10], sibling)

    r13, r17 = range(1, 4), range(1, 8)

    def small0():
        part_r = mm(up[...], g[...], 1, 1)
        for k in range(8):
            rank[k] = part_r[:, k * TOK:(k + 1) * TOK]
        rank_in[t] = rank[t]
        for d in r17:
            c_rank(d).start()
        cp_act.wait()
        total = jnp.zeros((HROWS, TOK), F32)
        step = 1024
        for c in range(WIDTH // step):
            cols = slice(c * step, (c + 1) * step)
            a_c = at[:, cols]
            hot = (iota((KOUT, step), 1) + c * step == idx[...]).astype(F32).astype(BF16)
            zero = jnp.zeros((HROWS - RANK - KOUT, step), BF16)
            basis = jnp.concatenate([a_c, hot, zero], axis=0)
            total = total + mm(basis, act[:, cols], 1, 1)
        hid[t] = total.astype(BF16)
        for d in r17:
            c_hid(d).start()

    def arrange():
        shuf = unshuffle()
        for c in range(8):
            groups = [at[:, (c * 8 + k) * GROUP:(c * 8 + k + 1) * GROUP] for k in range(8)]
            moved = mm(jnp.concatenate(groups, axis=0), shuf, 1, 1).astype(BF16)
            for k in range(8):
                lanes = slice((c * 8 + k) * GROUP, (c * 8 + k + 1) * GROUP)
                atp[:, lanes] = moved[k * RANK:(k + 1) * RANK]
        for k in range(4):
            gb[k * TOK:(k + 1) * TOK, :] = g[block(order[k], zh), :]

    def small1():
        for d in r17:
            c_rank(d).wait_recv()
        total = rank_in[0]
        for k in range(1, 8):
            total = total + rank_in[k]
        r_t = (2.0 * total).astype(BF16)
        r_v[...] = mm(eye(TOK), r_t, 1, 1).astype(BF16)
        for k in range(32):
            cols = slice(k * 256, (k + 1) * 256)
            dsum[k // 16, k % 16] = mm(r_t, act[:, cols], 1, 0)
        cd_core().start()

    def small2():
        for d in r17:
            c_hid(d).wait_recv()
        total = jnp.zeros((HROWS, FEATS), F32)
        for k in range(8):
            total = total + mm(hid[k], g[k * TOK:(k + 1) * TOK, :], 1, 0)
        for c in range(2):
            for k in range(4):
                usum[c, k] = total[k * 24:(k + 1) * 24, c * 384:(c + 1) * 384]
        cu_core().start()

    def small3():
        cd_core().wait_recv()
        for k in range(16):
            dsum[core, k] = dsum[core, k] + dbuf[k]
        for d in r13:
            cd_x(d).start()
        cu_core().wait_recv()
        for k in range(4):
            usum[core, k] = usum[core, k] + ubuf[k]
        for d in r13:
            cu_y(d).start()

    def small4():
        for d in r13:
            cd_x(d).wait_recv()
        for k in range(4):
            mine = dsum[core, x * 4 + k]
            for d in r13:
                mine = mine + dbuf[16 + 4 * (d - 1) + k]
            dsum[core, x * 4 + k] = mine
        for d in r13:
            cd_y(d).start()
        for d in r13:
            cu_y(d).wait_recv()
        mine = usum[core, y]
        for d in r13:
            mine = mine + ubuf[4 + d - 1]
        ubuf[7 + zl] = mine
        for d in r13:
            cu_z(d).start()

    def small5():
        for d in r13:
            cd_y(d).wait_recv()
        mine = dsum[core, x * 4 + y]
        for d in r13:
            mine = mine + dbuf[28 + d - 1]
        dbuf[31 + z] = mine
        for d in r17:
            cd_z(d).start()
        for d in r13:
            cu_z(d).wait_recv()
        total = ubuf[7]
        for k in r13:
            total = total + ubuf[7 + k]
        uall[core, y] = total
        for d in r13:
            cu_gy(d).start()

    def small6():
        for d in r17:
            cd_z(d).wait_recv()
        total = dbuf[31]
        for k in range(1, 8):
            total = total + dbuf[31 + k]
        dall[core, x * 4 + y] = total * NORM
        for d in r13:
            cd_gy(d).start()
        for d in r13:
            cu_gy(d).wait_recv()
        cu_gc().start()

    def small7():
        for d in r13:
            cd_gy(d).wait_recv()
        for d in r13:
            cd_gx(d).start()
        cu_gc().wait_recv()
        for c in range(2):
            lanes = slice(c * 384, (c + 1) * 384)
            u0 = uall[c, 0]
            out_u[:, lanes] = u0[:16] * (2.0 * NORM)
            out_o[0:8, lanes] = u0[16:] * NORM
            out_o[8:32, lanes] = uall[c, 1] * NORM
            out_o[32:56, lanes] = uall[c, 2] * NORM
            out_o[56:64, lanes] = uall[c, 3, :8] * NORM

    def small8():
        for d in r13:
            cd_gx(d).wait_recv()
        cd_gc().start()

    def small9():
        cd_gc().wait_recv()
        for c in range(2):
            for k in range(16):
                out_d[:, (c * 16 + k) * 256:(c * 16 + k + 1) * 256] = dall[c, k]

    unpack_a(0)
    cp_g.wait()
    stage1(0)
    pl.semaphore_wait(bar, len(peers))
    for i in range(2):
        c1(0, i).start()
    small0()
    for k in range(4):
        c_g(k).start()

    small = {0: arrange, 2: small1, 3: small2, 4: small3, 6: small4, 8: small5, 12: small6,
             14: small7, 15: small8, 16: small9}

    def batch(k, todo):
        hi = NB if k == len(CUTS) - 2 else CUTS[k + 1]
        lax.fori_loop(CUTS[k], hi, lambda b, c: (todo(b), c)[1], 0)

    def serve(n):
        for k in range(len(CUTS) - 1):
            for after, todo in ((2, weight_in), (1, weight_on), (0, weight_send)):
                pl.when(n == k + after)(functools.partial(batch, k, todo))

    def step(j, carry):
        j2, j3 = j - S2, j - S3
        pl.when((j2 >= 0) & (j2 < NA))(lambda: stage2(j2))
        pl.when((j2 >= NA) & (j2 < NC))(lambda: both2(j2 - NA))
        b = j - NA
        pl.when((b >= 0) & (b < NB))(lambda: weight_pair(b))
        serve(2 * (j - NA) + 3)
        pl.when((j3 >= 0) & (j3 < NA))(lambda: stage3(j3))
        pl.when(j3 >= NA)(lambda: both3(j3 - NA))

        @pl.when(j == NA - 2)
        def _():
            for k in range(4):
                c_g(k).wait_recv()

        serve(2 * (j - NA) + 4)

        @pl.when((j >= 1) & (j < NA))
        def _():
            unpack_a(j)
            stage1(j)
            for i in range(2):
                c1(j, i).start()

        ahead = 2 * j
        for k in range(2):
            pl.when((ahead >= 0) & (ahead + k < NB))(lambda: unpack_b(ahead + k))
        pl.when((j >= NA) & (j < NC))(lambda: both1(j - NA))

        late = j - NA - 1
        pl.when((late >= 0) & (late < NA))(lambda: cz(late).start())

        for at_step, todo in small.items():
            pl.when(j == at_step)(todo)
        return carry

    lax.fori_loop(0, NC + S3, step, 0)
    lax.fori_loop(0, NA, lambda a, c: (stage4(a), c)[1], 0)

    def drain_a(j, carry):
        for i in range(2):
            c1(j, i).wait_send()
            c2(j, i).wait_send()
        cz(j).wait_send()
        return carry

    def drain_b(b, carry):
        for i in range(2):
            d1(b, i).wait_send()
            d2(b, i).wait_send()
        for d in r13:
            c_wy(b, d).wait_send()
        c_wc(b).wait_send()


        @pl.when(outer)
        def _():
            c_wz(b).wait_send()
            c_wf(b).wait_send()

        return carry

    lax.fori_loop(0, NA, drain_a, 0)
    lax.fori_loop(0, NB, drain_b, 0)
    lax.fori_loop(0, NC, lambda j, c: (out_copy(j).wait(), c)[1], 0)
    for k in range(4):
        c_g(k).wait_send()
    for d in r17:
        c_rank(d).wait_send()
        c_hid(d).wait_send()
        cd_z(d).wait_send()
    for d in r13:
        cd_x(d).wait_send()
        cd_y(d).wait_send()
        cu_y(d).wait_send()
        cu_z(d).wait_send()
        cd_gy(d).wait_send()
        cd_gx(d).wait_send()
        cu_gy(d).wait_send()
    cd_core().wait_send()
    cu_core().wait_send()
    cd_gc().wait_send()
    cu_gc().wait_send()


def body(act, g, pk, scale, idx, dfw, a, up):
    hbm = pl.BlockSpec(memory_space=pl.ANY)
    vmem = pl.BlockSpec(memory_space=pltpu.VMEM)
    dma = pltpu.SemaphoreType.DMA
    out, d, u, o = pl.pallas_call(
        kernel,
        out_shape=(
            jax.ShapeDtypeStruct((TOK, WIDTH), BF16),
            jax.ShapeDtypeStruct((RANK, WIDTH), F32),
            jax.ShapeDtypeStruct((RANK, FEATS), F32),
            jax.ShapeDtypeStruct((KOUT, FEATS), F32),
        ),
        in_specs=[hbm, hbm, hbm, vmem, vmem, vmem, vmem, vmem],
        out_specs=(hbm, vmem, vmem, vmem),
        scratch_shapes=[
            pltpu.VMEM((TOK, WIDTH), BF16),
            pltpu.VMEM((8 * TOK, FEATS), BF16),
            pltpu.VMEM((4 * TOK, FEATS), BF16),
            pltpu.VMEM((4 * TOK, FEATS), BF16),
            pltpu.VMEM((NA, PR, FEATS), jnp.int32),
            pltpu.VMEM((PK, PR, FEATS), jnp.int32),
            pltpu.VMEM((KOUT, 1), jnp.int32),
            pltpu.VMEM((RANK, WIDTH), BF16),
            pltpu.VMEM((NC, DC, FEATS), BF16),
            pltpu.VMEM((NB, DC, FEATS), BF16),
            pltpu.VMEM((8, RANK, TOK), F32),
            pltpu.VMEM((8, RANK, TOK), F32),
            pltpu.VMEM((TOK, RANK), BF16),
            pltpu.VMEM((8, HROWS, TOK), BF16),
            pltpu.VMEM((2, 16, RANK, 256), F32),
            pltpu.VMEM((39, RANK, 256), F32),
            pltpu.VMEM((2, 16, RANK, 256), F32),
            pltpu.VMEM((2, 4, 24, 384), F32),
            pltpu.VMEM((11, 24, 384), F32),
            pltpu.VMEM((2, 4, 24, 384), F32),
            pltpu.VMEM((NA, 2, TOK, DC), BF16),
            pltpu.VMEM((NA, 2, TOK, DC), BF16),
            pltpu.VMEM((NA, 2, 2 * TOK, DC), BF16),
            pltpu.VMEM((NA, 2, 2 * TOK, DC), BF16),
            pltpu.VMEM((NA, TOK, DC), BF16),
            pltpu.VMEM((NA, TOK, DC), BF16),
            pltpu.VMEM((NA, TOK, DC), F32),
            pltpu.VMEM((NB, 2, TOK // 2, DC), BF16),
            pltpu.VMEM((NB, 2, TOK // 2, DC), BF16),
            pltpu.VMEM((NB, 2, TOK, DC), BF16),
            pltpu.VMEM((NB, 2, TOK, DC), BF16),
            pltpu.VMEM((S2 + 1, 2 * TOK, DC), F32),
            pltpu.VMEM((S3 + 1, TOK, DC), F32),
            pltpu.VMEM((NC, TOK, DC), BF16),
            dma((2,)), dma((NA,)), dma((PK,)), dma((NC,)),
            dma((NA, 2)), dma((NA, 2)), dma((NA, 2)), dma((NA, 2)),
            dma((NA,)), dma((NA,)),
            dma((NB, 2)), dma((NB, 2)), dma((NB, 2)), dma((NB, 2)),
            dma((4,)), dma((4,)),
            dma((NB,)), dma((NB,)), dma((NB,)), dma((NB, 3)), dma((NB, 3)), dma((NB,)), dma((NB,)),
            dma((8,)), dma((8,)), dma((8,)), dma((8,)),
            dma((21,)), dma((21,)), dma((11,)), dma((11,)),
        ],
        compiler_params=pltpu.CompilerParams(
            collective_id=0, has_side_effects=True, vmem_limit_bytes=62 << 20
        ),
        name="projection_backward",
    )(act, g, pk, scale, idx.reshape(1, KOUT), dfw, a.T, up)
    return out, d.T, u, o


def solution(mesh):
    tensor = P(None, "tensor")
    tokens = P(("dp", "tensor"), None)
    return jax.shard_map(
        body,
        mesh=mesh,
        in_specs=(tokens, P("dp", "tensor"), tensor, tensor, P(), tensor, P(), tensor),
        out_specs=(tokens, P(), tensor, tensor),
        check_vma=False,
    )
```

```python
import functools

import jax
import jax.numpy as jnp
from jax import lax
from jax.experimental import pallas as pl
from jax.experimental.pallas import tpu as pltpu
from jax.sharding import PartitionSpec as P

MESH = pl.DeviceIdType.MESH
F32 = jnp.float32
BF16 = jnp.bfloat16

WIDTH = 8192
FEATS = 768
RANK = 16
KOUT = 64
TOK = 128
GROUP = 128
DC = 512
NC = WIDTH // DC
GPC = DC // GROUP
PR = DC // 4
NA = 7
NB = NC - NA
S2 = 2
S3 = 4
CUTS = (0, 2, 5, 9)
PK = 6
HROWS = 96
NORM = 32768.0**-0.5


def mm(a, b, ca, cb):
    return lax.dot_general(a, b, (((ca,), (cb,)), ((), ())), preferred_element_type=F32)


def iota(shape, dim):
    return lax.broadcasted_iota(jnp.int32, shape, dim)


def eye(n):
    return (iota((n, n), 0) == iota((n, n), 1)).astype(BF16)


def unshuffle():
    q, d = iota((GROUP, GROUP), 0), iota((GROUP, GROUP), 1)
    return (d == 4 * (q & 31) + (q >> 5)).astype(BF16)


def kernel(
    act_h, g_h, pk_h, scale, idx_row, dfw, at, up,
    out_h, out_d, out_u, out_o,
    act, g, gb, gp, pka, pkb, idx, atp, w, wp, rank, rank_in, r_v, hid, dsum, dbuf, dall, usum, ubuf, uall,
    s1, r1, s2, r2, sz, rz, own, t1, q1, t2, q2, near, home, outv,
    l_sem, pka_sem, pkb_sem, o_sem, s1s, s1r, s2s, s2r, zs, zr, t1s, t1r, t2s, t2r, gs, gr,
    wzs, wzr, wfs, wys, wyr, wcs, wcr, rks, rkr, hs, hr, ds, dr, us, ur,
):
    dp = lax.axis_index("dp")
    t = lax.axis_index("tensor")
    core = lax.rem(dp, 2)
    y = dp // 8
    zl = lax.rem(dp // 2, 4)
    x = t // 2
    zh = lax.rem(t, 2)
    z = zh * 4 + zl

    def at_t(d):
        return (dp, lax.rem(t + d, 8))

    def at_x(d):
        return (dp, lax.rem(x + d + 4, 4) * 2 + zh)

    def at_y(d):
        return ((lax.rem(y + d, 4) * 4 + zl) * 2 + core, t)

    def at_z(d):
        zz = lax.rem(z + d, 8)
        return ((y * 4 + lax.rem(zz, 4)) * 2 + core, x * 2 + zz // 4)

    def at_zl(d):
        return ((y * 4 + lax.rem(zl + d, 4)) * 2 + core, t)

    sibling = (dp + 1 - 2 * core, t)

    def rc(src, dst, ssem, rsem, dev):
        return pltpu.make_async_remote_copy(
            src_ref=src, dst_ref=dst, send_sem=ssem, recv_sem=rsem,
            device_id=dev, device_id_type=MESH,
        )

    bar = pltpu.get_barrier_semaphore()
    peers = [at_t(d) for d in range(1, 8)]
    peers += [at_y(d) for d in range(1, 4)]
    peers += [at_z(d) for d in (1, 2, 3, 5, 6, 7)]
    peers += [sibling]
    for dev in peers:
        pl.semaphore_signal(bar, inc=1, device_id=dev, device_id_type=MESH)

    cp_g = pltpu.make_async_copy(g_h, g, l_sem.at[0])
    cp_act = pltpu.make_async_copy(act_h, act, l_sem.at[1])

    def cp_a(j):
        return pltpu.make_async_copy(pk_h.at[pl.ds(j * PR, PR)], pka.at[j], pka_sem.at[j])

    def cp_b(b):
        slot = lax.rem(b, PK)
        src = pk_h.at[pl.ds((NA + b) * PR, PR)]
        return pltpu.make_async_copy(src, pkb.at[slot], pkb_sem.at[slot])

    cp_g.start()
    cp_a(0).start()
    cp_b(0).start()
    for j in range(1, NA):
        cp_a(j).start()
    cp_act.start()
    for b in range(1, PK):
        cp_b(b).start()
    row = idx_row[...].astype(F32)
    idx[...] = jnp.sum(
        jnp.where(iota((KOUT, KOUT), 0) == iota((KOUT, KOUT), 1), row, 0.0),
        axis=1, keepdims=True,
    ).astype(jnp.int32)

    def unpack(j, packed):
        for q in range(GPC):
            k = j * GPC + q
            words = packed[pl.ds(q * 32, 32), :]
            srow = scale[pl.ds(k, 1), :]
            drow = dfw[pl.ds(k, 1), :]
            place = idx[pl.ds(k, 1), :] - k * GROUP
            place = (place & 3) * 32 + (place >> 2)
            for n in range(4):
                code = lax.shift_right_logical(words, 4 * n) & 15
                val = (code.astype(F32) - 8.0) * srow
                hit = iota((32, FEATS), 0) + n * 32 == place
                val = val + jnp.where(hit, drow, 0.0)
                w[j, pl.ds(q * GROUP + n * 32, 32), :] = val.astype(BF16)

    def unpack_a(j):
        cp_a(j).wait()
        unpack(j, pka.at[j])

    def unpack_b(b):
        cp_b(b).wait()
        unpack(NA + b, pkb.at[lax.rem(b, PK)])

        @pl.when(b + PK < NB)
        def _():
            cp_b(b + PK).start()

    def part(j, xx):
        rows = g[pl.ds(pl.multiple_of(xx * 256, 256), 256), :]
        return mm(rows, w[j], 1, 1)

    def c1(j, i):
        return rc(s1.at[j, i], r1.at[j, i], s1s.at[j, i], s1r.at[j, i], at_x(1 - 2 * i))

    def c2(j, i):
        return rc(s2.at[j, i], r2.at[j, i], s2s.at[j, i], s2r.at[j, i], at_x(1 - 2 * i))

    def cz(j):
        return rc(sz.at[j], rz.at[j], zs.at[j], zr.at[j], at_z(4))

    def stage1(j):
        p = part(j, lax.rem(x + 2, 4)).astype(BF16)
        s1[j, 0] = p[:TOK]
        s1[j, 1] = p[TOK:]

    def stage2(j):
        for i in range(2):
            p = part(j, lax.rem(x + 5 - 2 * i, 4))
            c1(j, i).wait_recv()
            got = r1[j, i].astype(F32)
            lo, hi = p[:TOK], p[TOK:]
            if i == 0:
                lo = lo + got
            else:
                hi = hi + got
            s2[j, i, pl.ds(0, TOK), :] = lo.astype(BF16)
            s2[j, i, pl.ds(TOK, TOK), :] = hi.astype(BF16)
            c2(j, i).start()

    def stage3(j):
        p = part(j, x)
        c2(j, 0).wait_recv()
        c2(j, 1).wait_recv()
        p = p + r2[j, 0].astype(F32) + r2[j, 1].astype(F32)
        first = zh == 0
        own[j] = jnp.where(first, p[:TOK], p[TOK:])
        sz[j] = jnp.where(first, p[TOK:], p[:TOK]).astype(BF16)

    def out_copy(j):
        cols = pl.ds(pl.multiple_of(j * DC, DC), DC)
        return pltpu.make_async_copy(outv.at[j], out_h.at[:, cols], o_sem.at[j])

    def finish(j, total):
        shuf = unshuffle()
        cols = atp[:, pl.ds(pl.multiple_of(j * DC, DC), DC)]
        full = (total + mm(r_v[...], cols, 1, 0)).astype(BF16)
        for q in range(GPC):
            lanes = slice(q * GROUP, (q + 1) * GROUP)
            outv[j, :, lanes] = mm(full[:, lanes], shuf, 1, 0).astype(BF16)
        out_copy(j).start()

    def stage4(j):
        cz(j).wait_recv()
        finish(j, own[j] + rz[j].astype(F32))

    order = (2, 1, 3, 0)

    def block(d, half):
        return pl.ds(pl.multiple_of((lax.rem(x + d, 4) * 2 + half) * TOK, TOK), TOK)

    def c_g(k):
        dst = gp.at[pl.ds(k * TOK, TOK)]
        return rc(g.at[block(order[k], 1 - zh)], dst, gs.at[k], gr.at[k], at_z(4))

    def piece(b, k):
        return wp.at[b, pl.ds(pl.multiple_of(core * 256 + k * 64, 64), 64)]

    outer = (zl == 0) | (zl == 3)

    def c_wz(b):
        src = w.at[NA + b, pl.ds(pl.multiple_of(core * 256 + y * 64, 64), 64)]
        return rc(src, piece(b, y), wzs.at[b], wzr.at[b], at_z(7 - 2 * zl))

    def c_wf(b):
        return rc(piece(b, y), piece(b, y), wfs.at[b], wzr.at[b], at_z(1 + 2 * zl))

    def c_wy(b, d):
        return rc(piece(b, y), piece(b, y), wys.at[b, d - 1], wyr.at[b, d - 1], at_y(d))

    def c_wc(b):
        ref = wp.at[b, pl.ds(pl.multiple_of(core * 256, 256), 256)]
        return rc(ref, ref, wcs.at[b], wcr.at[b], sibling)

    def spread(b):
        c_wz(b).wait_recv()
        for d in (1, 3, 2):
            c_wy(b, d).start()

    def weight_send(b):
        pl.when(outer)(lambda: c_wz(b).start())

    def weight_on(b):
        @pl.when(outer)
        def _():
            c_wz(b).wait_recv()
            c_wf(b).start()
            for d in (1, 3, 2):
                c_wy(b, d).start()

    def weight_in(b):
        pl.when(jnp.logical_not(outer))(lambda: spread(b))

    def weight_pair(b):
        for d in (1, 3, 2):
            c_wy(b, d).wait_recv()
        c_wc(b).start()

    def d1(b, i):
        return rc(t1.at[b, i], q1.at[b, i], t1s.at[b, i], t1r.at[b, i], at_x(1 - 2 * i))

    def d2(b, i):
        return rc(t2.at[b, i], q2.at[b, i], t2s.at[b, i], t2r.at[b, i], at_x(1 - 2 * i))

    def both1(b):
        c_wc(b).wait_recv()
        p = mm(gb[...], w[NA + b], 1, 1) + mm(gp[...], wp[b], 1, 1)
        far = p[:TOK].astype(BF16)
        t1[b, 0] = far[:64]
        t1[b, 1] = far[64:]
        near[lax.rem(b, S2 + 1)] = p[TOK:3 * TOK]
        home[lax.rem(b, S3 + 1)] = p[3 * TOK:]
        for i in range(2):
            d1(b, i).start()

    def both2(b):
        p = near[lax.rem(b, S2 + 1)]
        d1(b, 0).wait_recv()
        t2[b, 0, pl.ds(0, 64), :] = (p[:64] + q1[b, 0].astype(F32)).astype(BF16)
        t2[b, 0, pl.ds(64, 64), :] = p[64:128].astype(BF16)
        d2(b, 0).start()
        d1(b, 1).wait_recv()
        t2[b, 1, pl.ds(0, 64), :] = p[128:192].astype(BF16)
        t2[b, 1, pl.ds(64, 64), :] = (p[192:] + q1[b, 1].astype(F32)).astype(BF16)
        d2(b, 1).start()

    def both3(b):
        p = home[lax.rem(b, S3 + 1)]
        d2(b, 0).wait_recv()
        d2(b, 1).wait_recv()
        finish(NA + b, p + q2[b, 0].astype(F32) + q2[b, 1].astype(F32))

    def c_rank(d):
        return rc(rank.at[lax.rem(t + d, 8)], rank_in.at[t], rks.at[d], rkr.at[d], at_t(d))

    def c_hid(d):
        return rc(hid.at[t], hid.at[t], hs.at[d], hr.at[d], at_t(d))

    def cd_core():
        return rc(dsum.at[1 - core], dbuf.at[pl.ds(0, 16)], ds.at[0], dr.at[0], sibling)

    def cu_core():
        return rc(usum.at[1 - core], ubuf.at[pl.ds(0, 4)], us.at[0], ur.at[0], sibling)

    def cd_x(d):
        to = lax.rem(x + d, 4)
        src = dsum.at[core, pl.ds(to * 4, 4)]
        return rc(src, dbuf.at[pl.ds(16 + 4 * (d - 1), 4)], ds.at[d], dr.at[d], at_x(d))

    def cd_y(d):
        src = dsum.at[core, x * 4 + lax.rem(y + d, 4)]
        return rc(src, dbuf.at[28 + d - 1], ds.at[3 + d], dr.at[3 + d], at_y(d))

    def cd_z(d):
        return rc(dbuf.at[31 + z], dbuf.at[31 + z], ds.at[6 + d], dr.at[6 + d], at_z(d))

    def cu_y(d):
        src = usum.at[core, lax.rem(y + d, 4)]
        return rc(src, ubuf.at[4 + d - 1], us.at[d], ur.at[d], at_y(d))

    def cu_z(d):
        return rc(ubuf.at[7 + zl], ubuf.at[7 + zl], us.at[3 + d], ur.at[3 + d], at_zl(d))

    def cd_gy(d):
        ref = dall.at[core, x * 4 + y]
        return rc(ref, ref, ds.at[13 + d], dr.at[13 + d], at_y(d))

    def cd_gx(d):
        ref = dall.at[core, pl.ds(x * 4, 4)]
        return rc(ref, ref, ds.at[16 + d], dr.at[16 + d], at_x(d))

    def cd_gc():
        ref = dall.at[core]
        return rc(ref, ref, ds.at[20], dr.at[20], sibling)

    def cu_gy(d):
        ref = uall.at[core, y]
        return rc(ref, ref, us.at[6 + d], ur.at[6 + d], at_y(d))

    def cu_gc():
        ref = uall.at[core]
        return rc(ref, ref, us.at[10], ur.at[10], sibling)

    r13, r17 = range(1, 4), range(1, 8)

    def small0():
        part_r = mm(up[...], g[...], 1, 1)
        for k in range(8):
            rank[k] = part_r[:, k * TOK:(k + 1) * TOK]
        rank_in[t] = rank[t]
        cp_act.wait()
        total = jnp.zeros((HROWS, TOK), F32)
        step = 1024
        for c in range(WIDTH // step):
            cols = slice(c * step, (c + 1) * step)
            a_c = at[:, cols]
            hot = (iota((KOUT, step), 1) + c * step == idx[...]).astype(F32).astype(BF16)
            zero = jnp.zeros((HROWS - RANK - KOUT, step), BF16)
            basis = jnp.concatenate([a_c, hot, zero], axis=0)
            total = total + mm(basis, act[:, cols], 1, 1)
        hid[t] = total.astype(BF16)

    def arrange():
        shuf = unshuffle()
        for c in range(8):
            groups = [at[:, (c * 8 + k) * GROUP:(c * 8 + k + 1) * GROUP] for k in range(8)]
            moved = mm(jnp.concatenate(groups, axis=0), shuf, 1, 1).astype(BF16)
            for k in range(8):
                lanes = slice((c * 8 + k) * GROUP, (c * 8 + k + 1) * GROUP)
                atp[:, lanes] = moved[k * RANK:(k + 1) * RANK]
        for k in range(4):
            gb[k * TOK:(k + 1) * TOK, :] = g[block(order[k], zh), :]

    def small1():
        for d in r17:
            c_rank(d).wait_recv()
        total = rank_in[0]
        for k in range(1, 8):
            total = total + rank_in[k]
        r_t = (2.0 * total).astype(BF16)
        r_v[...] = mm(eye(TOK), r_t, 1, 1).astype(BF16)
        for k in range(32):
            cols = slice(k * 256, (k + 1) * 256)
            dsum[k // 16, k % 16] = mm(r_t, act[:, cols], 1, 0)
        cd_core().start()

    def small2():
        for d in r17:
            c_hid(d).wait_recv()
        total = jnp.zeros((HROWS, FEATS), F32)
        for k in range(8):
            total = total + mm(hid[k], g[k * TOK:(k + 1) * TOK, :], 1, 0)
        for c in range(2):
            for k in range(4):
                usum[c, k] = total[k * 24:(k + 1) * 24, c * 384:(c + 1) * 384]
        cu_core().start()

    def small3():
        cd_core().wait_recv()
        for k in range(16):
            dsum[core, k] = dsum[core, k] + dbuf[k]
        for d in r13:
            cd_x(d).start()
        cu_core().wait_recv()
        for k in range(4):
            usum[core, k] = usum[core, k] + ubuf[k]
        for d in r13:
            cu_y(d).start()

    def small4():
        for d in r13:
            cd_x(d).wait_recv()
        for k in range(4):
            mine = dsum[core, x * 4 + k]
            for d in r13:
                mine = mine + dbuf[16 + 4 * (d - 1) + k]
            dsum[core, x * 4 + k] = mine
        for d in r13:
            cd_y(d).start()
        for d in r13:
            cu_y(d).wait_recv()
        mine = usum[core, y]
        for d in r13:
            mine = mine + ubuf[4 + d - 1]
        ubuf[7 + zl] = mine
        for d in r13:
            cu_z(d).start()

    def small5():
        for d in r13:
            cd_y(d).wait_recv()
        mine = dsum[core, x * 4 + y]
        for d in r13:
            mine = mine + dbuf[28 + d - 1]
        dbuf[31 + z] = mine
        for d in r17:
            cd_z(d).start()
        for d in r13:
            cu_z(d).wait_recv()
        total = ubuf[7]
        for k in r13:
            total = total + ubuf[7 + k]
        uall[core, y] = total
        for d in r13:
            cu_gy(d).start()

    def small6():
        for d in r17:
            cd_z(d).wait_recv()
        total = dbuf[31]
        for k in range(1, 8):
            total = total + dbuf[31 + k]
        dall[core, x * 4 + y] = total * NORM
        for d in r13:
            cd_gy(d).start()
        for d in r13:
            cu_gy(d).wait_recv()
        cu_gc().start()

    def small7():
        for d in r13:
            cd_gy(d).wait_recv()
        for d in r13:
            cd_gx(d).start()
        cu_gc().wait_recv()
        for c in range(2):
            lanes = slice(c * 384, (c + 1) * 384)
            u0 = uall[c, 0]
            out_u[:, lanes] = u0[:16] * (2.0 * NORM)
            out_o[0:8, lanes] = u0[16:] * NORM
            out_o[8:32, lanes] = uall[c, 1] * NORM
            out_o[32:56, lanes] = uall[c, 2] * NORM
            out_o[56:64, lanes] = uall[c, 3, :8] * NORM

    def small8():
        for d in r13:
            cd_gx(d).wait_recv()
        cd_gc().start()

    def small9():
        cd_gc().wait_recv()
        for c in range(2):
            for k in range(16):
                out_d[:, (c * 16 + k) * 256:(c * 16 + k + 1) * 256] = dall[c, k]

    unpack_a(0)
    cp_g.wait()
    stage1(0)
    small0()
    pl.semaphore_wait(bar, len(peers))
    for i in range(2):
        c1(0, i).start()
    for d in r17:
        c_rank(d).start()
        c_hid(d).start()
    for k in range(4):
        c_g(k).start()

    small = {0: arrange, 2: small1, 3: small2, 4: small3, 6: small4, 8: small5, 12: small6,
             14: small7, 15: small8, 16: small9}

    def batch(k, todo):
        hi = NB if k == len(CUTS) - 2 else CUTS[k + 1]
        lax.fori_loop(CUTS[k], hi, lambda b, c: (todo(b), c)[1], 0)

    def serve(n):
        for k in range(len(CUTS) - 1):
            for after, todo in ((2, weight_in), (1, weight_on), (0, weight_send)):
                pl.when(n == k + after)(functools.partial(batch, k, todo))

    def step(j, carry):
        j2, j3 = j - S2, j - S3
        pl.when((j2 >= 0) & (j2 < NA))(lambda: stage2(j2))
        pl.when((j2 >= NA) & (j2 < NC))(lambda: both2(j2 - NA))
        b = j - NA
        pl.when((b >= 0) & (b < NB))(lambda: weight_pair(b))
        serve(2 * (j - NA) + 3)
        pl.when((j3 >= 0) & (j3 < NA))(lambda: stage3(j3))
        pl.when(j3 >= NA)(lambda: both3(j3 - NA))

        @pl.when(j == NA - 2)
        def _():
            for k in range(4):
                c_g(k).wait_recv()

        serve(2 * (j - NA) + 4)

        @pl.when((j >= 1) & (j < NA))
        def _():
            unpack_a(j)
            stage1(j)
            for i in range(2):
                c1(j, i).start()

        ahead = 2 * j
        for k in range(2):
            pl.when((ahead >= 0) & (ahead + k < NB))(lambda: unpack_b(ahead + k))
        pl.when((j >= NA) & (j < NC))(lambda: both1(j - NA))

        late = j - NA - 1
        pl.when((late >= 0) & (late < NA))(lambda: cz(late).start())

        for at_step, todo in small.items():
            pl.when(j == at_step)(todo)
        return carry

    lax.fori_loop(0, NC + S3, step, 0)
    lax.fori_loop(0, NA, lambda a, c: (stage4(a), c)[1], 0)

    def drain_a(j, carry):
        for i in range(2):
            c1(j, i).wait_send()
            c2(j, i).wait_send()
        cz(j).wait_send()
        return carry

    def drain_b(b, carry):
        for i in range(2):
            d1(b, i).wait_send()
            d2(b, i).wait_send()
        for d in r13:
            c_wy(b, d).wait_send()
        c_wc(b).wait_send()


        @pl.when(outer)
        def _():
            c_wz(b).wait_send()
            c_wf(b).wait_send()

        return carry

    lax.fori_loop(0, NA, drain_a, 0)
    lax.fori_loop(0, NB, drain_b, 0)
    lax.fori_loop(0, NC, lambda j, c: (out_copy(j).wait(), c)[1], 0)
    for k in range(4):
        c_g(k).wait_send()
    for d in r17:
        c_rank(d).wait_send()
        c_hid(d).wait_send()
        cd_z(d).wait_send()
    for d in r13:
        cd_x(d).wait_send()
        cd_y(d).wait_send()
        cu_y(d).wait_send()
        cu_z(d).wait_send()
        cd_gy(d).wait_send()
        cd_gx(d).wait_send()
        cu_gy(d).wait_send()
    cd_core().wait_send()
    cu_core().wait_send()
    cd_gc().wait_send()
    cu_gc().wait_send()


def body(act, g, pk, scale, idx, dfw, a, up):
    hbm = pl.BlockSpec(memory_space=pl.ANY)
    vmem = pl.BlockSpec(memory_space=pltpu.VMEM)
    dma = pltpu.SemaphoreType.DMA
    out, d, u, o = pl.pallas_call(
        kernel,
        out_shape=(
            jax.ShapeDtypeStruct((TOK, WIDTH), BF16),
            jax.ShapeDtypeStruct((RANK, WIDTH), F32),
            jax.ShapeDtypeStruct((RANK, FEATS), F32),
            jax.ShapeDtypeStruct((KOUT, FEATS), F32),
        ),
        in_specs=[hbm, hbm, hbm, vmem, vmem, vmem, vmem, vmem],
        out_specs=(hbm, vmem, vmem, vmem),
        scratch_shapes=[
            pltpu.VMEM((TOK, WIDTH), BF16),
            pltpu.VMEM((8 * TOK, FEATS), BF16),
            pltpu.VMEM((4 * TOK, FEATS), BF16),
            pltpu.VMEM((4 * TOK, FEATS), BF16),
            pltpu.VMEM((NA, PR, FEATS), jnp.int32),
            pltpu.VMEM((PK, PR, FEATS), jnp.int32),
            pltpu.VMEM((KOUT, 1), jnp.int32),
            pltpu.VMEM((RANK, WIDTH), BF16),
            pltpu.VMEM((NC, DC, FEATS), BF16),
            pltpu.VMEM((NB, DC, FEATS), BF16),
            pltpu.VMEM((8, RANK, TOK), F32),
            pltpu.VMEM((8, RANK, TOK), F32),
            pltpu.VMEM((TOK, RANK), BF16),
            pltpu.VMEM((8, HROWS, TOK), BF16),
            pltpu.VMEM((2, 16, RANK, 256), F32),
            pltpu.VMEM((39, RANK, 256), F32),
            pltpu.VMEM((2, 16, RANK, 256), F32),
            pltpu.VMEM((2, 4, 24, 384), F32),
            pltpu.VMEM((11, 24, 384), F32),
            pltpu.VMEM((2, 4, 24, 384), F32),
            pltpu.VMEM((NA, 2, TOK, DC), BF16),
            pltpu.VMEM((NA, 2, TOK, DC), BF16),
            pltpu.VMEM((NA, 2, 2 * TOK, DC), BF16),
            pltpu.VMEM((NA, 2, 2 * TOK, DC), BF16),
            pltpu.VMEM((NA, TOK, DC), BF16),
            pltpu.VMEM((NA, TOK, DC), BF16),
            pltpu.VMEM((NA, TOK, DC), F32),
            pltpu.VMEM((NB, 2, TOK // 2, DC), BF16),
            pltpu.VMEM((NB, 2, TOK // 2, DC), BF16),
            pltpu.VMEM((NB, 2, TOK, DC), BF16),
            pltpu.VMEM((NB, 2, TOK, DC), BF16),
            pltpu.VMEM((S2 + 1, 2 * TOK, DC), F32),
            pltpu.VMEM((S3 + 1, TOK, DC), F32),
            pltpu.VMEM((NC, TOK, DC), BF16),
            dma((2,)), dma((NA,)), dma((PK,)), dma((NC,)),
            dma((NA, 2)), dma((NA, 2)), dma((NA, 2)), dma((NA, 2)),
            dma((NA,)), dma((NA,)),
            dma((NB, 2)), dma((NB, 2)), dma((NB, 2)), dma((NB, 2)),
            dma((4,)), dma((4,)),
            dma((NB,)), dma((NB,)), dma((NB,)), dma((NB, 3)), dma((NB, 3)), dma((NB,)), dma((NB,)),
            dma((8,)), dma((8,)), dma((8,)), dma((8,)),
            dma((21,)), dma((21,)), dma((11,)), dma((11,)),
        ],
        compiler_params=pltpu.CompilerParams(
            collective_id=0, has_side_effects=True, vmem_limit_bytes=62 << 20
        ),
        name="projection_backward",
    )(act, g, pk, scale, idx.reshape(1, KOUT), dfw, a.T, up)
    return out, d.T, u, o


def solution(mesh):
    tensor = P(None, "tensor")
    tokens = P(("dp", "tensor"), None)
    return jax.shard_map(
        body,
        mesh=mesh,
        in_specs=(tokens, P("dp", "tensor"), tensor, tensor, P(), tensor, P(), tensor),
        out_specs=(tokens, P(), tensor, tensor),
        check_vma=False,
    )
```
